32 devices in a mesh: hours: 8 (over y, x, core), blocks: 4 (over z).
Axes of the slice: x: 2, y: 2, z: 4, core: 2. Of those that a mesh axis runs over, the one named last changes fastest.
Arguments:
- spectra: float32 [8, 64, 3, 2, 2048], P('hours', 'blocks'), may hold values from -6 to 6
- validity: int32 [8, 64], P('hours', 'blocks'), may hold values from 0 to 1, as said below
Outputs:
- near_stack: float32 [4, 2, 2304, 256], P('blocks', None, 'hours')
- far_stack: float32 [4, 1152, 256], P('blocks', 'hours')
The draws below stay inside these ranges and needn't reach their ends.
Inputs may be any that keep to these rules, and one draw needn't show every extreme that they name: `validity`: 0 or 1; some stations are invalid in every hour.
All inputs are finite; a program needn't handle non-finite values.
Results may differ from the reference program's by a relative error of at most 0.0058.
Values may be sent and summed in bfloat16 or wider, within the bound.
A program may use at most 64 MiB of HBM per device.

```python
import math
import jax
import jax.numpy as jnp
from jax import lax

FREQS = 2048
BAND = 128
LAGS = 256
COMPS = 3
SB = 16
STATIONS = 64
HOURS = 8
N_BLOCKS = 4


def draw_validity(key, part):
    first_key, second_key, third_key = jax.random.split(key, 3)
    hour_index = jnp.arange(HOURS, dtype=jnp.int32)[:, None]
    threshold = 20 + 44 * hour_index // max(HOURS - 1, 1)
    rolled = jax.random.randint(first_key, (HOURS, STATIONS), 0, 64)
    alive = rolled < threshold
    outage = jax.random.randint(second_key, (1, STATIONS), 0, 16) == 0
    chosen = jax.random.randint(third_key, (1, 1), 0, STATIONS)
    outage = outage | (jnp.arange(STATIONS, dtype=jnp.int32)[None, :] == chosen)
    return jnp.where(alive & jnp.logical_not(outage), 1, 0).astype(jnp.int32)


def levels(own_key, extent, pieces, low, largest):
    gain = 1.0
    for position, parts in pieces:
        steps = jax.random.uniform(jax.random.fold_in(jax.random.fold_in(own_key, 6), position), (parts,), jnp.float32, low / len(pieces), largest / len(pieces))
        gain = gain * jnp.repeat(jnp.exp(steps), extent[position] // parts).reshape((-1,) + (1,) * (len(extent) - 1 - position))
    return gain


def normal_values(key, shape, scale, most, shards=(), kind=jnp.bfloat16):
    values = jax.random.normal(key, shape, jnp.float32) * scale
    if len(shards) > 0:
        values = levels(key, shape, shards, -0.22, 0.18) * values
    return jnp.clip(values, min=-most, max=most).astype(kind)


def setup_inputs(seed: int = 0) -> dict:
    seeds = jax.random.split(jax.random.key(seed), 3)
    spectra = normal_values(seeds[0], (HOURS, STATIONS, COMPS, 2, FREQS), 1.0, 6.0, ((0, 8), (1, 4)), jnp.float32)
    validity = draw_validity(jax.random.fold_in(seeds[2], 71), 0)
    return {"spectra": spectra, "validity": validity}


EPSILON = 1e-06

def whiten(spectra, validity, band_width):
    hour_count, station_count, comp_count, part_count, freq_count = spectra.shape
    grouped = spectra.reshape(hour_count, station_count, comp_count, part_count, freq_count // band_width, band_width)
    band_power = lax.optimization_barrier(jnp.mean(grouped * grouped, axis=(3, 5), keepdims=True))
    valid_f = validity.astype(jnp.float32).reshape(hour_count, station_count, 1, 1, 1, 1)
    scaled = grouped * (valid_f / jnp.sqrt(band_power + EPSILON))
    return scaled.reshape(hour_count, station_count * comp_count, part_count, freq_count).astype(jnp.bfloat16)

def build_table(freq_count, lag_count):
    freq_index = jnp.arange(freq_count, dtype=jnp.int32)[:, None]
    lag_index = jnp.arange(lag_count, dtype=jnp.int32)[None, :] - lag_count // 2
    residue = freq_index * (lag_index + 2 * freq_count) % (2 * freq_count)
    angles = residue.astype(jnp.float32) * (math.pi / freq_count)
    amplitude = 8.0 / math.sqrt(freq_count)
    return jnp.concatenate([jnp.cos(angles) * amplitude, -jnp.sin(angles) * amplitude], 0).astype(jnp.bfloat16)

def cross_spectrum(row_block, col_block):
    row_real = row_block[..., :, None, 0, :].astype(jnp.float32)
    row_imag = row_block[..., :, None, 1, :].astype(jnp.float32)
    col_real = col_block[..., None, :, 0, :].astype(jnp.float32)
    col_imag = col_block[..., None, :, 1, :].astype(jnp.float32)
    real_part = row_real * col_real + row_imag * col_imag
    imag_part = row_imag * col_real - row_real * col_imag
    stacked_parts = jnp.stack([real_part, imag_part], -2)
    dims_shape = stacked_parts.shape
    return stacked_parts.reshape(dims_shape[:-4] + (dims_shape[-4] * dims_shape[-3], dims_shape[-2] * dims_shape[-1])).astype(jnp.bfloat16)

def expand(counts, comp_count):
    return jnp.repeat(jnp.repeat(counts, comp_count, 0), comp_count, 1).reshape(-1)

def reference(spectra, validity):
    white = whiten(spectra, validity, BAND)
    table = build_table(FREQS, LAGS).astype(jnp.float32)
    valid_f = validity.astype(jnp.float32)
    pair_counts = jnp.dot(valid_f.T, valid_f, precision=lax.Precision.HIGHEST)
    trace_count = COMPS * SB
    half_width = trace_count // 2
    block_count = N_BLOCKS
    near_rounds = block_count // 2

    def stacked(row_start, row_count, col_start):
        row_block = white[:, row_start:row_start + row_count]
        col_block = white[:, col_start:col_start + trace_count]

        def add_hour(running, hour_pair):
            return (running + cross_spectrum(hour_pair[0], hour_pair[1]).astype(jnp.float32), None)
        running, unused = lax.scan(add_hour, jnp.zeros((row_count * trace_count, 2 * FREQS), jnp.float32), (row_block, col_block))
        correlogram = jnp.dot(running, table, precision=lax.Precision.HIGHEST)
        sub_block = pair_counts[row_start // COMPS:(row_start + row_count) // COMPS, col_start // COMPS:col_start // COMPS + SB]
        valid_hours = expand(sub_block, COMPS)
        return correlogram / jnp.maximum(valid_hours, 1.0)[:, None]
    near_list = []
    far_list = []
    for my_block in range(block_count):
        near_list.append(jnp.stack([stacked(my_block * trace_count, trace_count, (my_block - round_index) % block_count * trace_count) for round_index in range(near_rounds)], 0))
        partner = (my_block + near_rounds) % block_count
        if my_block < near_rounds:
            far_list.append(stacked(my_block * trace_count, half_width, partner * trace_count))
        else:
            far_list.append(stacked(partner * trace_count + half_width, half_width, my_block * trace_count))
    return (jnp.stack(near_list, 0), jnp.stack(far_list, 0))
```

```python
import functools
import math

import jax
import jax.numpy as jnp
import ml_dtypes
import numpy as np
from jax import lax
from jax.experimental import pallas as pl
from jax.experimental.pallas import tpu as pltpu
from jax.sharding import PartitionSpec as P

BAND = 128
LAGS = 256
EPSILON = 1e-06
CHUNK = 256


def passed_along(block, axis, distance):
    devices = range(lax.axis_size(axis))
    route = [((i - distance) % len(devices), i) for i in devices]
    return lax.ppermute(block, axis, route)


def chunked_table(freq_count, lag_count):
    freq = np.arange(freq_count, dtype=np.int64)[:, None]
    lag = np.arange(lag_count, dtype=np.int64)[None, :] - lag_count // 2
    angles = ((freq * lag) % (2 * freq_count)).astype(np.float64) * (math.pi / freq_count)
    amplitude = 8.0 / math.sqrt(freq_count)
    parts = np.stack([np.cos(angles) * amplitude, -np.sin(angles) * amplitude], 0)
    parts = parts.reshape(2, freq_count // CHUNK, CHUNK, lag_count).transpose(1, 0, 2, 3)
    return parts.reshape(2 * freq_count, lag_count).astype(np.float32).astype(ml_dtypes.bfloat16)


def whiten_into(spectra_ref, valid_ref, store):
    freq_count = spectra_ref.shape[2]
    valid = valid_ref[...]
    for band in range(freq_count // BAND):
        lanes = slice(band * BAND, (band + 1) * BAND)
        real = spectra_ref[:, 0, lanes]
        imag = spectra_ref[:, 1, lanes]
        total = jnp.sum(real * real + imag * imag, axis=1, keepdims=True)
        scale = valid / jnp.sqrt(total * (1.0 / (2 * BAND)) + EPSILON)
        store(0, lanes, (real * scale).astype(jnp.bfloat16))
        store(1, lanes, (imag * scale).astype(jnp.bfloat16))


def whiten_kernel(spectra_ref, valid_ref, white_ref):
    def store(part, lanes, value):
        white_ref[part, :, lanes] = value

    whiten_into(spectra_ref, valid_ref, store)


def cross_chunk(rows_ref, row_start, row_count, cols_ref, panel, chunk, out_ref):
    col_count = cols_ref.shape[2]
    lanes = pl.ds(chunk * CHUNK, CHUNK)
    cols = [
        (
            cols_ref[panel, 0, q : q + 16, lanes],
            cols_ref[panel, 1, q : q + 16, lanes],
        )
        for q in range(0, col_count, 16)
    ]
    for a in range(row_count):
        row_real = jnp.broadcast_to(rows_ref[0, pl.ds(row_start + a, 1), lanes], (16, CHUNK))
        row_imag = jnp.broadcast_to(rows_ref[1, pl.ds(row_start + a, 1), lanes], (16, CHUNK))
        row_real = row_real.astype(jnp.bfloat16)
        row_imag = row_imag.astype(jnp.bfloat16)
        for q, (col_real, col_imag) in enumerate(cols):
            at = slice(a * col_count + q * 16, a * col_count + q * 16 + 16)
            out_ref[at, :CHUNK] = row_real * col_real + row_imag * col_imag
            out_ref[at, CHUNK:] = row_imag * col_real - row_real * col_imag


def correlate_unit(rows_ref, row_start, row_count, cols_ref, panel, table_ref, acc_ref, tiles):
    chunk_count = rows_ref.shape[2] // CHUNK
    cross = functools.partial(cross_chunk, rows_ref, row_start, row_count, cols_ref, panel)
    cross(0, tiles[0])
    for chunk in range(chunk_count):
        if chunk + 1 < chunk_count:
            cross(chunk + 1, tiles[(chunk + 1) % 2])
        term = jnp.dot(
            tiles[chunk % 2][...],
            table_ref[chunk * 2 * CHUNK : (chunk + 1) * 2 * CHUNK, :],
            preferred_element_type=jnp.float32,
        )
        if chunk == 0:
            acc_ref[...] = term
        else:
            acc_ref[...] += term


def correlate_kernel(block_count, white_ref, table_ref, out_ref, rows, tile0, tile1):
    trace_count = white_ref.shape[2]
    half = trace_count // 2
    is_lower = lax.axis_index("blocks") < block_count // 2
    rows[:, :trace_count, :] = white_ref[0].astype(jnp.float32)
    far_own = white_ref[0, :, :, :].astype(jnp.float32)[:, :half]
    far_other = white_ref[2, :, :, :].astype(jnp.float32)[:, half:]
    rows[:, trace_count:, :] = jnp.where(is_lower, far_own, far_other)

    def one_unit(unit, carry):
        near = unit < 4
        row_start = jnp.where(near, lax.rem(unit, 2) * half, trace_count)
        panel = jnp.where(near, unit // 2, jnp.where(is_lower, 2, 0))
        correlate_unit(
            rows, row_start, half, white_ref, panel, table_ref, out_ref.at[unit], (tile0, tile1)
        )
        return carry

    lax.fori_loop(0, 5, one_unit, 0)


def expand(counts, comp_count):
    return jnp.repeat(jnp.repeat(counts, comp_count, 0), comp_count, 1).reshape(-1)


def on_device(table, spectra, validity):
    hour_count, station_count, comp_count, part_count, freq_count = spectra.shape
    trace_count = station_count * comp_count
    half_width = trace_count // 2
    half_stations = station_count // 2
    block_count = lax.axis_size("blocks")
    near_rounds = block_count // 2
    my_block = lax.axis_index("blocks")
    is_lower = my_block < near_rounds
    valid_f = jnp.repeat(validity.reshape(-1).astype(jnp.float32), comp_count)[:, None]
    white = pl.pallas_call(
        whiten_kernel,
        out_shape=jax.ShapeDtypeStruct((part_count, trace_count, freq_count), jnp.bfloat16),
        in_specs=[pl.BlockSpec(memory_space=pltpu.VMEM)] * 2,
        out_specs=pl.BlockSpec(memory_space=pltpu.VMEM),
    )(spectra.reshape(trace_count, part_count, freq_count), valid_f)
    panels = [white] + [passed_along(white, "blocks", r) for r in range(1, near_rounds + 1)]
    pair_rows = half_width * trace_count
    sums = pl.pallas_call(
        functools.partial(correlate_kernel, block_count),
        out_shape=jax.ShapeDtypeStruct((5, pair_rows, LAGS), jnp.float32),
        in_specs=[pl.BlockSpec(memory_space=pltpu.VMEM)] * 2,
        out_specs=pl.BlockSpec(memory_space=pltpu.VMEM),
        scratch_shapes=[
            pltpu.VMEM((part_count, trace_count + half_width, freq_count), jnp.float32),
            pltpu.VMEM((pair_rows, 2 * CHUNK), jnp.bfloat16),
            pltpu.VMEM((pair_rows, 2 * CHUNK), jnp.bfloat16),
        ],
        compiler_params=pltpu.CompilerParams(vmem_limit_bytes=56 * 1024 * 1024),
    )(jnp.stack(panels, 0), table)
    near_terms = sums[:4].reshape(near_rounds, 2 * pair_rows, LAGS)
    far_terms = sums[4]
    hour_devices = lax.axis_size("hours")
    share_near = trace_count * trace_count // hour_devices
    share_far = half_width * trace_count // hour_devices
    my_slot = lax.axis_index("hours")
    hour_masks = lax.all_gather(validity, "hours", axis=0, tiled=True)
    all_masks = lax.all_gather(hour_masks, "blocks", axis=1, tiled=True).astype(jnp.float32)
    pair_counts = jnp.dot(
        all_masks.T, all_masks, precision=lax.Precision.HIGHEST, preferred_element_type=jnp.float32
    )
    near_sum, far_sum = (
        lax.psum_scatter(near_terms, "hours", scatter_dimension=1, tiled=True),
        lax.psum_scatter(far_terms, "hours", scatter_dimension=0, tiled=True),
    )

    def block_count_of(row_start, row_count, col_start):
        sub_block = lax.dynamic_slice(
            pair_counts, (row_start, col_start), (row_count, station_count)
        )
        return expand(sub_block, comp_count)

    near_full = jnp.stack(
        [
            block_count_of(
                my_block * station_count,
                station_count,
                (my_block - round_index) % block_count * station_count,
            )
            for round_index in range(near_rounds)
        ],
        0,
    )
    far_partner = (my_block + near_rounds) % block_count
    far_full = block_count_of(
        jnp.where(is_lower, my_block * station_count, far_partner * station_count + half_stations),
        half_stations,
        jnp.where(is_lower, far_partner, my_block) * station_count,
    )
    near_count = lax.dynamic_slice_in_dim(near_full, my_slot * share_near, share_near, 1)
    far_count = lax.dynamic_slice_in_dim(far_full, my_slot * share_far, share_far, 0)
    near_stack = near_sum / jnp.maximum(near_count, 1.0)[..., None]
    far_stack = far_sum / jnp.maximum(far_count, 1.0)[..., None]
    return (near_stack[None], far_stack[None])


def solution(mesh):
    in_specs = (P("hours", "blocks", None, None, None), P("hours", "blocks"))
    out_specs = (P("blocks", None, "hours", None), P("blocks", "hours", None))

    def run(spectra, validity):
        table = chunked_table(spectra.shape[-1], LAGS)
        return jax.shard_map(
            lambda *args: on_device(jnp.asarray(table), *args),
            mesh=mesh, in_specs=in_specs, out_specs=out_specs, check_vma=False,
        )(spectra, validity)

    return run
```

```python
import functools
import math

import jax
import jax.numpy as jnp
import ml_dtypes
import numpy as np
from jax import lax
from jax.experimental import pallas as pl
from jax.experimental.pallas import tpu as pltpu
from jax.sharding import PartitionSpec as P

BAND = 128
LAGS = 256
EPSILON = 1e-06
CHUNK = 256


def passed_along(block, axis, distance):
    devices = range(lax.axis_size(axis))
    route = [((i - distance) % len(devices), i) for i in devices]
    return lax.ppermute(block, axis, route)


def chunked_table(freq_count, lag_count):
    freq = np.arange(freq_count, dtype=np.int64)[:, None]
    lag = np.arange(lag_count, dtype=np.int64)[None, :] - lag_count // 2
    angles = ((freq * lag) % (2 * freq_count)).astype(np.float64) * (math.pi / freq_count)
    amplitude = 8.0 / math.sqrt(freq_count)
    parts = np.stack([np.cos(angles) * amplitude, -np.sin(angles) * amplitude], 0)
    parts = parts.reshape(2, freq_count // CHUNK, CHUNK, lag_count).transpose(1, 0, 2, 3)
    return parts.reshape(2 * freq_count, lag_count).astype(np.float32).astype(ml_dtypes.bfloat16)


def whiten_into(spectra_ref, valid_ref, store):
    freq_count = spectra_ref.shape[2]
    valid = valid_ref[...]
    for band in range(freq_count // BAND):
        lanes = slice(band * BAND, (band + 1) * BAND)
        real = spectra_ref[:, 0, lanes]
        imag = spectra_ref[:, 1, lanes]
        total = jnp.sum(real * real + imag * imag, axis=1, keepdims=True)
        scale = valid / jnp.sqrt(total * (1.0 / (2 * BAND)) + EPSILON)
        store(0, lanes, (real * scale).astype(jnp.bfloat16))
        store(1, lanes, (imag * scale).astype(jnp.bfloat16))


def whiten_kernel(spectra_ref, valid_ref, white_ref):
    def store(part, lanes, value):
        white_ref[part, :, lanes] = value

    whiten_into(spectra_ref, valid_ref, store)


def cross_chunk(rows_ref, row_start, row_count, cols_ref, panel, chunk, out_ref):
    col_count = cols_ref.shape[2]
    lanes = pl.ds(chunk * CHUNK, CHUNK)
    cols = [
        (
            cols_ref[panel, 0, q : q + 16, lanes],
            cols_ref[panel, 1, q : q + 16, lanes],
        )
        for q in range(0, col_count, 16)
    ]
    for a in range(row_count):
        row_real = jnp.broadcast_to(rows_ref[0, pl.ds(row_start + a, 1), lanes], (16, CHUNK))
        row_imag = jnp.broadcast_to(rows_ref[1, pl.ds(row_start + a, 1), lanes], (16, CHUNK))
        row_real = row_real.astype(jnp.bfloat16)
        row_imag = row_imag.astype(jnp.bfloat16)
        for q, (col_real, col_imag) in enumerate(cols):
            at = slice(a * col_count + q * 16, a * col_count + q * 16 + 16)
            out_ref[at, :CHUNK] = row_real * col_real + row_imag * col_imag
            out_ref[at, CHUNK:] = row_imag * col_real - row_real * col_imag


def correlate_unit(rows_ref, row_start, row_count, cols_ref, panel, table_ref, acc_ref, tiles):
    chunk_count = rows_ref.shape[2] // CHUNK
    cross = functools.partial(cross_chunk, rows_ref, row_start, row_count, cols_ref, panel)
    cross(0, tiles[0])
    for chunk in range(chunk_count):
        if chunk + 1 < chunk_count:
            cross(chunk + 1, tiles[(chunk + 1) % 2])
        term = jnp.dot(
            tiles[chunk % 2][...],
            table_ref[chunk * 2 * CHUNK : (chunk + 1) * 2 * CHUNK, :],
            preferred_element_type=jnp.float32,
        )
        if chunk == 0:
            acc_ref[...] = term
        else:
            acc_ref[...] += term


def correlate_kernel(block_count, white_ref, table_ref, out_ref, rows, tile0, tile1):
    trace_count = white_ref.shape[2]
    half = trace_count // 2
    is_lower = lax.axis_index("blocks") < block_count // 2
    rows[:, :trace_count, :] = white_ref[0].astype(jnp.float32)
    far_own = white_ref[0, :, :, :].astype(jnp.float32)[:, :half]
    far_other = white_ref[2, :, :, :].astype(jnp.float32)[:, half:]
    rows[:, trace_count:, :] = jnp.where(is_lower, far_own, far_other)

    def one_unit(unit, carry):
        near = unit < 4
        row_start = jnp.where(near, lax.rem(unit, 2) * half, trace_count)
        panel = jnp.where(near, unit // 2, jnp.where(is_lower, 2, 0))
        correlate_unit(
            rows, row_start, half, white_ref, panel, table_ref, out_ref.at[unit], (tile0, tile1)
        )
        return carry

    lax.fori_loop(0, 5, one_unit, 0)


def expand(counts, comp_count):
    return jnp.repeat(jnp.repeat(counts, comp_count, 0), comp_count, 1).reshape(-1)


def on_device(table, spectra, validity):
    hour_count, station_count, comp_count, part_count, freq_count = spectra.shape
    trace_count = station_count * comp_count
    half_width = trace_count // 2
    half_stations = station_count // 2
    block_count = lax.axis_size("blocks")
    near_rounds = block_count // 2
    my_block = lax.axis_index("blocks")
    is_lower = my_block < near_rounds
    valid_f = jnp.repeat(validity.reshape(-1).astype(jnp.float32), comp_count)[:, None]
    white = pl.pallas_call(
        whiten_kernel,
        out_shape=jax.ShapeDtypeStruct((part_count, trace_count, freq_count), jnp.bfloat16),
        in_specs=[pl.BlockSpec(memory_space=pltpu.VMEM)] * 2,
        out_specs=pl.BlockSpec(memory_space=pltpu.VMEM),
    )(spectra.reshape(trace_count, part_count, freq_count), valid_f)
    panels = [white] + [passed_along(white, "blocks", r) for r in range(1, near_rounds + 1)]
    pair_rows = half_width * trace_count
    sums = pl.pallas_call(
        functools.partial(correlate_kernel, block_count),
        out_shape=jax.ShapeDtypeStruct((5, pair_rows, LAGS), jnp.float32),
        in_specs=[pl.BlockSpec(memory_space=pltpu.VMEM)] * 2,
        out_specs=pl.BlockSpec(memory_space=pltpu.VMEM),
        scratch_shapes=[
            pltpu.VMEM((part_count, trace_count + half_width, freq_count), jnp.float32),
            pltpu.VMEM((pair_rows, 2 * CHUNK), jnp.bfloat16),
            pltpu.VMEM((pair_rows, 2 * CHUNK), jnp.bfloat16),
        ],
        compiler_params=pltpu.CompilerParams(vmem_limit_bytes=56 * 1024 * 1024),
    )(jnp.stack(panels, 0), table)
    near_terms = sums[:4].reshape(near_rounds, 2 * pair_rows, LAGS)
    far_terms = sums[4]
    hour_devices = lax.axis_size("hours")
    share_near = trace_count * trace_count // hour_devices
    share_far = half_width * trace_count // hour_devices
    my_slot = lax.axis_index("hours")
    hour_masks = lax.all_gather(validity, "hours", axis=0, tiled=True)
    all_masks = lax.all_gather(hour_masks, "blocks", axis=1, tiled=True).astype(jnp.float32)
    pair_counts = jnp.dot(
        all_masks.T, all_masks, precision=lax.Precision.HIGHEST, preferred_element_type=jnp.float32
    )
    near_sum, far_sum = (
        lax.psum_scatter(near_terms, "hours", scatter_dimension=1, tiled=True),
        lax.psum_scatter(far_terms, "hours", scatter_dimension=0, tiled=True),
    )

    def block_count_of(row_start, row_count, col_start):
        sub_block = lax.dynamic_slice(
            pair_counts, (row_start, col_start), (row_count, station_count)
        )
        return expand(sub_block, comp_count)

    near_full = jnp.stack(
        [
            block_count_of(
                my_block * station_count,
                station_count,
                (my_block - round_index) % block_count * station_count,
            )
            for round_index in range(near_rounds)
        ],
        0,
    )
    far_partner = (my_block + near_rounds) % block_count
    far_full = block_count_of(
        jnp.where(is_lower, my_block * station_count, far_partner * station_count + half_stations),
        half_stations,
        jnp.where(is_lower, far_partner, my_block) * station_count,
    )
    near_count = lax.dynamic_slice_in_dim(near_full, my_slot * share_near, share_near, 1)
    far_count = lax.dynamic_slice_in_dim(far_full, my_slot * share_far, share_far, 0)
    near_stack = near_sum / jnp.maximum(near_count, 1.0)[..., None]
    far_stack = far_sum / jnp.maximum(far_count, 1.0)[..., None]
    return (near_stack[None], far_stack[None])


def fused_kernel(
    sizes, spectra_ref, valid_ref, tile_ref, table_ref, near_ref, far_ref,
    white, rows, tile0, tile1, acc, masks, all_masks,
    near_part, far_part, near_sib, far_sib, near_pair, far_pair, near_in, far_in,
    z_send, z_recv, m_send, m_recv, h_send, h_recv, s_send, s_recv, c_send, c_recv,
):
    block_count, hour_devices = sizes
    chips = hour_devices // 2
    trace_count = white.shape[2]
    half = trace_count // 2
    near_share = near_ref.shape[1]
    far_share = far_ref.shape[0]
    me = lax.axis_index("hours")
    block = lax.axis_index("blocks")
    core = lax.rem(me, 2)
    chip = me // 2
    other = 1 - core
    is_lower = block < block_count // 2
    following = lax.rem(block + 1, block_count)
    partner = lax.rem(block + 2, block_count)

    def remote(src, dst, send, recv, device):
        return pltpu.make_async_remote_copy(
            src_ref=src, dst_ref=dst, send_sem=send, recv_sem=recv,
            device_id=device, device_id_type=pl.DeviceIdType.MESH,
        )

    barrier = pltpu.get_barrier_semaphore()
    for step in range(1, hour_devices):
        pl.semaphore_signal(
            barrier, inc=1, device_id={"hours": lax.rem(me + step, hour_devices)},
            device_id_type=pl.DeviceIdType.MESH,
        )
    for step in range(1, block_count):
        pl.semaphore_signal(
            barrier, inc=1, device_id={"blocks": lax.rem(block + step, block_count)},
            device_id_type=pl.DeviceIdType.MESH,
        )

    def store(part, lanes, value):
        white[0, part, :, lanes] = value
        rows[part, :trace_count, lanes] = value.astype(jnp.float32)

    whiten_into(spectra_ref, valid_ref, store)
    masks[0] = tile_ref[...]
    pl.semaphore_wait(barrier, hour_devices + block_count - 2)

    mask_copies = [
        remote(masks.at[0], masks.at[i + 1], m_send.at[i], m_recv.at[i], {"blocks": to})
        for i, to in enumerate((following, partner))
    ]
    near_copy = remote(
        white.at[0], white.at[1], z_send.at[0], z_recv.at[0], {"blocks": following}
    )
    full_copy = remote(
        white.at[0], white.at[2], z_send.at[1], z_recv.at[1], {"blocks": partner}
    )
    lead = half // 16 * 16
    upper_part = pl.ds(lead, trace_count - lead)
    half_copy = remote(
        white.at[0, :, upper_part], white.at[2, :, upper_part],
        z_send.at[1], z_recv.at[1], {"blocks": partner},
    )
    for copy in mask_copies:
        copy.start()
    near_copy.start()

    @pl.when(is_lower)
    def _():
        half_copy.start()

    @pl.when(jnp.logical_not(is_lower))
    def _():
        full_copy.start()

    def hour_copy(step):
        return remote(
            masks, all_masks.at[me], h_send.at[step - 1], h_recv.at[step - 1],
            {"hours": lax.rem(me + step, hour_devices)},
        )

    def sibling_near(unit):
        at = pl.ds(lax.rem(unit, 2) * (chips // 2), chips // 2)
        r = unit // 2
        return remote(
            near_part.at[r, other, at], near_sib.at[r, at],
            s_send.at[unit], s_recv.at[unit], {"hours": chip * 2 + other},
        )

    sibling_far = remote(
        far_part.at[other], far_sib, s_send.at[4], s_recv.at[4], {"hours": chip * 2 + other}
    )

    def chip_near(r, target):
        return remote(
            near_pair.at[r, target], near_in.at[r, chip],
            c_send.at[r, target], c_recv.at[r, chip], {"hours": target * 2 + core},
        )

    def chip_far(target):
        return remote(
            far_pair.at[target], far_in.at[chip],
            c_send.at[2, target], c_recv.at[2, chip], {"hours": target * 2 + core},
        )

    def reduce_near(unit):
        sibling_near(unit).wait_recv()
        r = unit // 2
        for i in range(chips // 2):
            target = lax.rem(unit, 2) * (chips // 2) + i

            @pl.when(target != chip)
            def _():
                near_pair[r, target] = (
                    near_part[r, core, target].astype(jnp.float32)
                    + near_sib[r, target].astype(jnp.float32)
                ).astype(jnp.bfloat16)
                chip_near(r, target).start()

    def one_unit(unit, carry):
        near = unit < 4

        @pl.when(unit == 2)
        def _():
            for copy in mask_copies:
                copy.wait_recv()
            all_masks[me] = masks[...]
            for step in range(1, hour_devices):
                hour_copy(step).start()
            near_copy.wait_recv()

        @pl.when(jnp.logical_and(unit == 4, is_lower))
        def _():
            full_copy.wait_recv()
            rows[:, trace_count:, :] = rows[:, :half, :]

        @pl.when(jnp.logical_and(unit == 4, jnp.logical_not(is_lower)))
        def _():
            half_copy.wait_recv()
            for part in range(2):
                value = white[2, part, lead:, :].astype(jnp.float32)
                rows[part, trace_count:, :] = value[half - lead :]

        row_start = jnp.where(near, lax.rem(unit, 2) * half, trace_count)
        panel = jnp.where(near, unit // 2, jnp.where(is_lower, 2, 0))
        correlate_unit(rows, row_start, half, white, panel, table_ref, acc, (tile0, tile1))

        @pl.when(near)
        def _():
            for i in range(hour_devices // 2):
                target = lax.rem(unit, 2) * (chips // 2) + i // 2
                near_part[unit // 2, i % 2, target] = acc[
                    i * near_share : (i + 1) * near_share, :
                ].astype(jnp.bfloat16)
            sibling_near(unit).start()

        @pl.when(jnp.logical_not(near))
        def _():
            for i in range(hour_devices):
                far_part[i % 2, i // 2] = acc[
                    i * far_share : (i + 1) * far_share, :
                ].astype(jnp.bfloat16)
            sibling_far.start()

        @pl.when(unit >= 1)
        def _():
            reduce_near(unit - 1)

        return carry

    lax.fori_loop(0, 5, one_unit, 0)

    sibling_far.wait_recv()
    for step in range(1, chips):
        target = lax.rem(chip + step, chips)
        far_pair[target] = (
            far_part[core, target].astype(jnp.float32) + far_sib[target].astype(jnp.float32)
        ).astype(jnp.bfloat16)
        chip_far(target).start()

    for step in range(1, hour_devices):
        hour_copy(step).wait()

    def counts(row_mask, row_start, row_count, col_mask):
        shape = (row_count, trace_count, 128)
        lane = lax.broadcasted_iota(jnp.int32, shape, 2)
        row = lax.broadcasted_iota(jnp.int32, shape, 0) + row_start
        col = lax.broadcasted_iota(jnp.int32, shape, 1)
        flat = (row_count * trace_count, 128)

        def picked(index, mask):
            chosen = jnp.where(lane == index, 1.0, 0.0).reshape(flat)
            return lax.dot_general(
                chosen, mask, (((1,), (1,)), ((), ())), preferred_element_type=jnp.float32
            )

        both = picked(row, row_mask) * picked(col, col_mask)
        return jnp.maximum(jnp.sum(both, axis=1, keepdims=True), 1.0)

    row_share = near_share // trace_count
    own_mask = all_masks[:, 0, 0, :]
    near_counts = [
        counts(own_mask, me * row_share, row_share, all_masks[:, r, 0, :]) for r in range(2)
    ]
    far_mask = all_masks[:, 2, 0, :]
    far_count = counts(
        jnp.where(is_lower, own_mask, far_mask),
        me * (row_share // 2) + jnp.where(is_lower, 0, half),
        row_share // 2,
        jnp.where(is_lower, far_mask, own_mask),
    )

    def chip_near_arrival(r, source):
        return remote(
            near_pair.at[r, source], near_in.at[r, source],
            c_send.at[r, source], c_recv.at[r, source], {"hours": source * 2 + core},
        )

    def chip_far_arrival(source):
        return remote(
            far_pair.at[source], far_in.at[source],
            c_send.at[2, source], c_recv.at[2, source], {"hours": source * 2 + core},
        )

    for r in range(2):
        total = near_part[r, core, chip].astype(jnp.float32) + near_sib[r, chip].astype(
            jnp.float32
        )
        for step in range(1, chips):
            source = lax.rem(chip + step, chips)
            chip_near_arrival(r, source).wait()
            total = total + near_in[r, source].astype(jnp.float32)
        near_ref[r] = total / near_counts[r]
    total = far_part[core, chip].astype(jnp.float32) + far_sib[chip].astype(jnp.float32)
    for step in range(1, chips):
        source = lax.rem(chip + step, chips)
        chip_far_arrival(source).wait()
        total = total + far_in[source].astype(jnp.float32)
    far_ref[...] = total / far_count

    for copy in mask_copies:
        copy.wait_send()
    near_copy.wait_send()

    @pl.when(is_lower)
    def _():
        half_copy.wait_send()

    @pl.when(jnp.logical_not(is_lower))
    def _():
        full_copy.wait_send()

    for unit in range(4):
        sibling_near(unit).wait_send()
    sibling_far.wait_send()


def on_device_fused(table, spectra, validity):
    hour_count, station_count, comp_count, part_count, freq_count = spectra.shape
    trace_count = station_count * comp_count
    half = trace_count // 2
    block_count = lax.axis_size("blocks")
    hour_devices = lax.axis_size("hours")
    chips = hour_devices // 2
    pair_rows = half * trace_count
    near_share = 2 * pair_rows // hour_devices
    far_share = pair_rows // hour_devices
    valid_f = jnp.repeat(validity.reshape(-1).astype(jnp.float32), comp_count)
    tile = jnp.broadcast_to(jnp.pad(valid_f, (0, 128 - trace_count))[None, :], (8, 128))
    near, far = pl.pallas_call(
        functools.partial(fused_kernel, (block_count, hour_devices)),
        out_shape=(
            jax.ShapeDtypeStruct((2, near_share, LAGS), jnp.float32),
            jax.ShapeDtypeStruct((far_share, LAGS), jnp.float32),
        ),
        in_specs=[pl.BlockSpec(memory_space=pltpu.VMEM)] * 4,
        out_specs=[pl.BlockSpec(memory_space=pltpu.VMEM)] * 2,
        scratch_shapes=[
            pltpu.VMEM((3, part_count, trace_count, freq_count), jnp.bfloat16),
            pltpu.VMEM((part_count, trace_count + half, freq_count), jnp.float32),
            pltpu.VMEM((pair_rows, 2 * CHUNK), jnp.bfloat16),
            pltpu.VMEM((pair_rows, 2 * CHUNK), jnp.bfloat16),
            pltpu.VMEM((pair_rows, LAGS), jnp.float32),
            pltpu.VMEM((3, 8, 128), jnp.float32),
            pltpu.VMEM((hour_devices, 3, 8, 128), jnp.float32),
            pltpu.VMEM((2, 2, chips, near_share, LAGS), jnp.bfloat16),
            pltpu.VMEM((2, chips, far_share, LAGS), jnp.bfloat16),
            pltpu.VMEM((2, chips, near_share, LAGS), jnp.bfloat16),
            pltpu.VMEM((chips, far_share, LAGS), jnp.bfloat16),
            pltpu.VMEM((2, chips, near_share, LAGS), jnp.bfloat16),
            pltpu.VMEM((chips, far_share, LAGS), jnp.bfloat16),
            pltpu.VMEM((2, chips, near_share, LAGS), jnp.bfloat16),
            pltpu.VMEM((chips, far_share, LAGS), jnp.bfloat16),
            pltpu.SemaphoreType.DMA((2,)),
            pltpu.SemaphoreType.DMA((2,)),
            pltpu.SemaphoreType.DMA((2,)),
            pltpu.SemaphoreType.DMA((2,)),
            pltpu.SemaphoreType.DMA((hour_devices - 1,)),
            pltpu.SemaphoreType.DMA((hour_devices - 1,)),
            pltpu.SemaphoreType.DMA((5,)),
            pltpu.SemaphoreType.DMA((5,)),
            pltpu.SemaphoreType.DMA((3, chips)),
            pltpu.SemaphoreType.DMA((3, chips)),
        ],
        compiler_params=pltpu.CompilerParams(
            vmem_limit_bytes=48 * 1024 * 1024, collective_id=0, has_side_effects=True
        ),
    )(spectra.reshape(trace_count, part_count, freq_count), valid_f[:, None], tile, table)
    return near[None], far[None]


def solution(mesh):
    in_specs = (P("hours", "blocks", None, None, None), P("hours", "blocks"))
    out_specs = (P("blocks", None, "hours", None), P("blocks", "hours", None))

    def run(spectra, validity):
        table = chunked_table(spectra.shape[-1], LAGS)
        fits = mesh.shape["hours"] == 8 and mesh.shape["blocks"] == 4
        device_part = on_device_fused if fits else on_device
        return jax.shard_map(
            lambda *args: device_part(jnp.asarray(table), *args),
            mesh=mesh, in_specs=in_specs, out_specs=out_specs, check_vma=False,
        )(spectra, validity)

    return run
```

```python
import functools
import math

import jax
import jax.numpy as jnp
import ml_dtypes
import numpy as np
from jax import lax
from jax.experimental import pallas as pl
from jax.experimental.pallas import tpu as pltpu
from jax.sharding import PartitionSpec as P

BAND = 128
LAGS = 256
EPSILON = 1e-06
CHUNK = 256


def passed_along(block, axis, distance):
    devices = range(lax.axis_size(axis))
    route = [((i - distance) % len(devices), i) for i in devices]
    return lax.ppermute(block, axis, route)


def chunked_table(freq_count, lag_count):
    freq = np.arange(freq_count, dtype=np.int64)[:, None]
    lag = np.arange(lag_count, dtype=np.int64)[None, :] - lag_count // 2
    angles = ((freq * lag) % (2 * freq_count)).astype(np.float64) * (math.pi / freq_count)
    amplitude = 8.0 / math.sqrt(freq_count)
    parts = np.stack([np.cos(angles) * amplitude, -np.sin(angles) * amplitude], 0)
    parts = parts.reshape(2, freq_count // CHUNK, CHUNK, lag_count).transpose(1, 0, 2, 3)
    return parts.reshape(2 * freq_count, lag_count).astype(np.float32).astype(ml_dtypes.bfloat16)


def whiten_into(spectra_ref, valid_ref, store):
    freq_count = spectra_ref.shape[2]
    valid = valid_ref[...]
    for band in range(freq_count // BAND):
        lanes = slice(band * BAND, (band + 1) * BAND)
        real = spectra_ref[:, 0, lanes]
        imag = spectra_ref[:, 1, lanes]
        total = jnp.sum(real * real + imag * imag, axis=1, keepdims=True)
        scale = valid / jnp.sqrt(total * (1.0 / (2 * BAND)) + EPSILON)
        store(0, lanes, (real * scale).astype(jnp.bfloat16))
        store(1, lanes, (imag * scale).astype(jnp.bfloat16))


def whiten_kernel(spectra_ref, valid_ref, white_ref):
    def store(part, lanes, value):
        white_ref[part, :, lanes] = value

    whiten_into(spectra_ref, valid_ref, store)


def cross_chunk(rows_ref, row_start, row_count, cols_ref, panel, chunk, out_ref):
    col_count = cols_ref.shape[2]
    lanes = pl.ds(chunk * CHUNK, CHUNK)
    cols = [
        (
            cols_ref[panel, 0, q : q + 16, lanes],
            cols_ref[panel, 1, q : q + 16, lanes],
        )
        for q in range(0, col_count, 16)
    ]
    for a in range(row_count):
        row_real = jnp.broadcast_to(rows_ref[0, pl.ds(row_start + a, 1), lanes], (16, CHUNK))
        row_imag = jnp.broadcast_to(rows_ref[1, pl.ds(row_start + a, 1), lanes], (16, CHUNK))
        row_real = row_real.astype(jnp.bfloat16)
        row_imag = row_imag.astype(jnp.bfloat16)
        for q, (col_real, col_imag) in enumerate(cols):
            at = slice(a * col_count + q * 16, a * col_count + q * 16 + 16)
            out_ref[at, :CHUNK] = row_real * col_real + row_imag * col_imag
            out_ref[at, CHUNK:] = row_imag * col_real - row_real * col_imag


def correlate_unit(rows_ref, row_start, row_count, cols_ref, panel, table_ref, acc_ref, tiles):
    chunk_count = rows_ref.shape[2] // CHUNK
    cross = functools.partial(cross_chunk, rows_ref, row_start, row_count, cols_ref, panel)
    cross(0, tiles[0])
    for chunk in range(chunk_count):
        if chunk + 1 < chunk_count:
            cross(chunk + 1, tiles[(chunk + 1) % 2])
        term = jnp.dot(
            tiles[chunk % 2][...],
            table_ref[chunk * 2 * CHUNK : (chunk + 1) * 2 * CHUNK, :],
            preferred_element_type=jnp.float32,
        )
        if chunk == 0:
            acc_ref[...] = term
        else:
            acc_ref[...] += term


def correlate_kernel(block_count, white_ref, table_ref, out_ref, rows, tile0, tile1):
    trace_count = white_ref.shape[2]
    half = trace_count // 2
    is_lower = lax.axis_index("blocks") < block_count // 2
    rows[:, :trace_count, :] = white_ref[0].astype(jnp.float32)
    far_own = white_ref[0, :, :, :].astype(jnp.float32)[:, :half]
    far_other = white_ref[2, :, :, :].astype(jnp.float32)[:, half:]
    rows[:, trace_count:, :] = jnp.where(is_lower, far_own, far_other)

    def one_unit(unit, carry):
        near = unit < 4
        row_start = jnp.where(near, lax.rem(unit, 2) * half, trace_count)
        panel = jnp.where(near, unit // 2, jnp.where(is_lower, 2, 0))
        correlate_unit(
            rows, row_start, half, white_ref, panel, table_ref, out_ref.at[unit], (tile0, tile1)
        )
        return carry

    lax.fori_loop(0, 5, one_unit, 0)


def expand(counts, comp_count):
    return jnp.repeat(jnp.repeat(counts, comp_count, 0), comp_count, 1).reshape(-1)


def on_device(table, spectra, validity):
    hour_count, station_count, comp_count, part_count, freq_count = spectra.shape
    trace_count = station_count * comp_count
    half_width = trace_count // 2
    half_stations = station_count // 2
    block_count = lax.axis_size("blocks")
    near_rounds = block_count // 2
    my_block = lax.axis_index("blocks")
    is_lower = my_block < near_rounds
    valid_f = jnp.repeat(validity.reshape(-1).astype(jnp.float32), comp_count)[:, None]
    white = pl.pallas_call(
        whiten_kernel,
        out_shape=jax.ShapeDtypeStruct((part_count, trace_count, freq_count), jnp.bfloat16),
        in_specs=[pl.BlockSpec(memory_space=pltpu.VMEM)] * 2,
        out_specs=pl.BlockSpec(memory_space=pltpu.VMEM),
    )(spectra.reshape(trace_count, part_count, freq_count), valid_f)
    panels = [white] + [passed_along(white, "blocks", r) for r in range(1, near_rounds + 1)]
    pair_rows = half_width * trace_count
    sums = pl.pallas_call(
        functools.partial(correlate_kernel, block_count),
        out_shape=jax.ShapeDtypeStruct((5, pair_rows, LAGS), jnp.float32),
        in_specs=[pl.BlockSpec(memory_space=pltpu.VMEM)] * 2,
        out_specs=pl.BlockSpec(memory_space=pltpu.VMEM),
        scratch_shapes=[
            pltpu.VMEM((part_count, trace_count + half_width, freq_count), jnp.float32),
            pltpu.VMEM((pair_rows, 2 * CHUNK), jnp.bfloat16),
            pltpu.VMEM((pair_rows, 2 * CHUNK), jnp.bfloat16),
        ],
        compiler_params=pltpu.CompilerParams(vmem_limit_bytes=56 * 1024 * 1024),
    )(jnp.stack(panels, 0), table)
    near_terms = sums[:4].reshape(near_rounds, 2 * pair_rows, LAGS)
    far_terms = sums[4]
    hour_devices = lax.axis_size("hours")
    share_near = trace_count * trace_count // hour_devices
    share_far = half_width * trace_count // hour_devices
    my_slot = lax.axis_index("hours")
    hour_masks = lax.all_gather(validity, "hours", axis=0, tiled=True)
    all_masks = lax.all_gather(hour_masks, "blocks", axis=1, tiled=True).astype(jnp.float32)
    pair_counts = jnp.dot(
        all_masks.T, all_masks, precision=lax.Precision.HIGHEST, preferred_element_type=jnp.float32
    )
    near_sum, far_sum = (
        lax.psum_scatter(near_terms, "hours", scatter_dimension=1, tiled=True),
        lax.psum_scatter(far_terms, "hours", scatter_dimension=0, tiled=True),
    )

    def block_count_of(row_start, row_count, col_start):
        sub_block = lax.dynamic_slice(
            pair_counts, (row_start, col_start), (row_count, station_count)
        )
        return expand(sub_block, comp_count)

    near_full = jnp.stack(
        [
            block_count_of(
                my_block * station_count,
                station_count,
                (my_block - round_index) % block_count * station_count,
            )
            for round_index in range(near_rounds)
        ],
        0,
    )
    far_partner = (my_block + near_rounds) % block_count
    far_full = block_count_of(
        jnp.where(is_lower, my_block * station_count, far_partner * station_count + half_stations),
        half_stations,
        jnp.where(is_lower, far_partner, my_block) * station_count,
    )
    near_count = lax.dynamic_slice_in_dim(near_full, my_slot * share_near, share_near, 1)
    far_count = lax.dynamic_slice_in_dim(far_full, my_slot * share_far, share_far, 0)
    near_stack = near_sum / jnp.maximum(near_count, 1.0)[..., None]
    far_stack = far_sum / jnp.maximum(far_count, 1.0)[..., None]
    return (near_stack[None], far_stack[None])


def fused_kernel(
    sizes, spectra_ref, valid_ref, tile_ref, table_hbm, near_ref, far_ref,
    table_ref, white, rows, tile0, tile1, acc, masks, all_masks,
    near_part, far_part, near_sib, far_sib, near_pair, far_pair, near_in, far_in,
    z_send, z_recv, f_send, t_sem, m_send, m_recv, h_send, h_recv, s_send, s_recv,
    c_send, c_recv,
):
    block_count, hour_devices = sizes
    chips = hour_devices // 2
    trace_count = white.shape[2]
    half = trace_count // 2
    near_share = near_ref.shape[1]
    far_share = far_ref.shape[0]
    me = lax.axis_index("hours")
    block = lax.axis_index("blocks")
    core = lax.rem(me, 2)
    chip = me // 2
    other = 1 - core
    is_lower = block < block_count // 2
    following = lax.rem(block + 1, block_count)
    partner = lax.rem(block + 2, block_count)

    def remote(src, dst, send, recv, device):
        return pltpu.make_async_remote_copy(
            src_ref=src, dst_ref=dst, send_sem=send, recv_sem=recv,
            device_id=device, device_id_type=pl.DeviceIdType.MESH,
        )

    table_copy = pltpu.make_async_copy(table_hbm, table_ref, t_sem)
    table_copy.start()
    barrier = pltpu.get_barrier_semaphore()
    for step in range(1, hour_devices):
        pl.semaphore_signal(
            barrier, inc=1, device_id={"hours": lax.rem(me + step, hour_devices)},
            device_id_type=pl.DeviceIdType.MESH,
        )
    for step in range(1, block_count):
        pl.semaphore_signal(
            barrier, inc=1, device_id={"blocks": lax.rem(block + step, block_count)},
            device_id_type=pl.DeviceIdType.MESH,
        )

    def store(part, lanes, value):
        white[0, part, :, lanes] = value
        rows[part, :trace_count, lanes] = value.astype(jnp.float32)

    whiten_into(spectra_ref, valid_ref, store)
    masks[0] = tile_ref[...]
    pl.semaphore_wait(barrier, hour_devices + block_count - 2)

    mask_copies = [
        remote(masks.at[0], masks.at[i + 1], m_send.at[i], m_recv.at[i], {"blocks": to})
        for i, to in enumerate((following, partner))
    ]
    lead = half // 16 * 16
    upper_part = pl.ds(lead, trace_count - lead)
    parts = range(2)
    near_copies = [
        remote(
            white.at[0, p], white.at[1, p], z_send.at[p], z_recv.at[p], {"blocks": following}
        )
        for p in parts
    ]
    full_copies = [
        remote(
            white.at[0, p], white.at[2, p], z_send.at[2 + p], z_recv.at[2 + p],
            {"blocks": partner},
        )
        for p in parts
    ]
    half_copies = [
        remote(
            white.at[0, p, upper_part], white.at[2, p, upper_part],
            z_send.at[2 + p], z_recv.at[2 + p], {"blocks": partner},
        )
        for p in parts
    ]
    last = block == block_count - 1
    relay = block == 1
    relay_copies = [
        remote(
            white.at[2, p], white.at[1, p], f_send.at[p], z_recv.at[p],
            {"blocks": lax.rem(block + block_count - 1, block_count)},
        )
        for p in parts
    ]
    for copy in mask_copies:
        copy.start()

    @pl.when(last)
    def _():
        for copy in full_copies:
            copy.start()

    @pl.when(jnp.logical_not(last))
    def _():
        for copy in near_copies:
            copy.start()

    def relay_part(p):
        @pl.when(relay)
        def _():
            full_copies[p].wait_recv()
            relay_copies[p].start()

    table_copy.wait()

    def hour_copy(step):
        return remote(
            masks, all_masks.at[me], h_send.at[step - 1], h_recv.at[step - 1],
            {"hours": lax.rem(me + step, hour_devices)},
        )

    def sibling_near(unit):
        at = pl.ds((unit % 2) * (chips // 2), chips // 2)
        r = unit // 2
        return remote(
            near_part.at[r, other, at], near_sib.at[r, at],
            s_send.at[unit], s_recv.at[unit], {"hours": chip * 2 + other},
        )

    sibling_far = remote(
        far_part.at[other], far_sib, s_send.at[4], s_recv.at[4], {"hours": chip * 2 + other}
    )

    def chip_near(r, target):
        return remote(
            near_pair.at[r, target], near_in.at[r, chip],
            c_send.at[r, target], c_recv.at[r, chip], {"hours": target * 2 + core},
        )

    def chip_far(target):
        return remote(
            far_pair.at[target], far_in.at[chip],
            c_send.at[2, target], c_recv.at[2, chip], {"hours": target * 2 + core},
        )

    def reduce_near(unit):
        sibling_near(unit).wait_recv()
        r = unit // 2
        for i in range(chips // 2):
            target = (unit % 2) * (chips // 2) + i

            @pl.when(target != chip)
            def _():
                near_pair[r, target] = (
                    near_part[r, core, target].astype(jnp.float32)
                    + near_sib[r, target].astype(jnp.float32)
                ).astype(jnp.bfloat16)
                chip_near(r, target).start()

    def one_unit(unit, carry):
        near = unit < 4

        @pl.when(unit == 1)
        def _():
            relay_part(0)

        @pl.when(unit == 2)
        def _():
            relay_part(1)

            @pl.when(is_lower)
            def _():
                for copy in half_copies:
                    copy.start()

            @pl.when(jnp.logical_not(jnp.logical_or(is_lower, last)))
            def _():
                for copy in full_copies:
                    copy.start()

            for copy in mask_copies:
                copy.wait_recv()
            all_masks[me] = masks[...]
            for step in range(1, hour_devices):
                hour_copy(step).start()
            reduce_near(1)
            for copy in near_copies:
                copy.wait_recv()

        @pl.when(unit == 4)
        def _():
            reduce_near(3)

            @pl.when(block == 0)
            def _():
                for copy in full_copies:
                    copy.wait_recv()

            @pl.when(is_lower)
            def _():
                rows[:, trace_count:, :] = rows[:, :half, :]

            @pl.when(jnp.logical_not(is_lower))
            def _():
                for p in parts:
                    half_copies[p].wait_recv()
                    value = white[2, p, lead:, :].astype(jnp.float32)
                    rows[p, trace_count:, :] = value[half - lead :]

        row_start = jnp.where(near, lax.rem(unit, 2) * half, trace_count)
        panel = jnp.where(near, unit // 2, jnp.where(is_lower, 2, 0))
        correlate_unit(rows, row_start, half, white, panel, table_ref, acc, (tile0, tile1))

        @pl.when(near)
        def _():
            for i in range(hour_devices // 2):
                target = lax.rem(unit, 2) * (chips // 2) + i // 2
                near_part[unit // 2, i % 2, target] = acc[
                    i * near_share : (i + 1) * near_share, :
                ].astype(jnp.bfloat16)
            sibling_near(unit).start()

        @pl.when(jnp.logical_not(near))
        def _():
            for i in range(hour_devices):
                far_part[i % 2, i // 2] = acc[
                    i * far_share : (i + 1) * far_share, :
                ].astype(jnp.bfloat16)
            sibling_far.start()

        @pl.when(jnp.logical_or(unit == 1, unit == 3))
        def _():
            reduce_near(unit - 1)

        return carry

    lax.fori_loop(0, 5, one_unit, 0)

    sibling_far.wait_recv()
    for step in range(1, chips):
        target = lax.rem(chip + step, chips)
        far_pair[target] = (
            far_part[core, target].astype(jnp.float32) + far_sib[target].astype(jnp.float32)
        ).astype(jnp.bfloat16)
        chip_far(target).start()

    for step in range(1, hour_devices):
        hour_copy(step).wait()

    def counts(row_mask, row_start, row_count, col_mask):
        shape = (row_count, trace_count, 128)
        lane = lax.broadcasted_iota(jnp.int32, shape, 2)
        row = lax.broadcasted_iota(jnp.int32, shape, 0) + row_start
        col = lax.broadcasted_iota(jnp.int32, shape, 1)
        flat = (row_count * trace_count, 128)

        def picked(index, mask):
            chosen = jnp.where(lane == index, 1.0, 0.0).reshape(flat)
            return lax.dot_general(
                chosen, mask, (((1,), (1,)), ((), ())), preferred_element_type=jnp.float32
            )

        both = picked(row, row_mask) * picked(col, col_mask)
        return jnp.maximum(jnp.sum(both, axis=1, keepdims=True), 1.0)

    row_share = near_share // trace_count
    own_mask = all_masks[:, 0, 0, :]
    near_counts = [
        counts(own_mask, me * row_share, row_share, all_masks[:, r, 0, :]) for r in range(2)
    ]
    far_mask = all_masks[:, 2, 0, :]
    far_count = counts(
        jnp.where(is_lower, own_mask, far_mask),
        me * (row_share // 2) + jnp.where(is_lower, 0, half),
        row_share // 2,
        jnp.where(is_lower, far_mask, own_mask),
    )

    def chip_near_arrival(r, source):
        return remote(
            near_pair.at[r, source], near_in.at[r, source],
            c_send.at[r, source], c_recv.at[r, source], {"hours": source * 2 + core},
        )

    def chip_far_arrival(source):
        return remote(
            far_pair.at[source], far_in.at[source],
            c_send.at[2, source], c_recv.at[2, source], {"hours": source * 2 + core},
        )

    for r in range(2):
        total = near_part[r, core, chip].astype(jnp.float32) + near_sib[r, chip].astype(
            jnp.float32
        )
        for step in range(1, chips):
            source = lax.rem(chip + step, chips)
            chip_near_arrival(r, source).wait()
            total = total + near_in[r, source].astype(jnp.float32)
        near_ref[r] = total / near_counts[r]
    total = far_part[core, chip].astype(jnp.float32) + far_sib[chip].astype(jnp.float32)
    for step in range(1, chips):
        source = lax.rem(chip + step, chips)
        chip_far_arrival(source).wait()
        total = total + far_in[source].astype(jnp.float32)
    far_ref[...] = total / far_count

    for copy in mask_copies:
        copy.wait_send()

    @pl.when(jnp.logical_not(last))
    def _():
        for copy in near_copies:
            copy.wait_send()

    @pl.when(relay)
    def _():
        for copy in relay_copies:
            copy.wait_send()

    @pl.when(is_lower)
    def _():
        for copy in half_copies:
            copy.wait_send()

    @pl.when(jnp.logical_not(is_lower))
    def _():
        for copy in full_copies:
            copy.wait_send()

    for unit in range(4):
        sibling_near(unit).wait_send()
    sibling_far.wait_send()


def on_device_fused(table, spectra, validity):
    hour_count, station_count, comp_count, part_count, freq_count = spectra.shape
    trace_count = station_count * comp_count
    half = trace_count // 2
    block_count = lax.axis_size("blocks")
    hour_devices = lax.axis_size("hours")
    chips = hour_devices // 2
    pair_rows = half * trace_count
    near_share = 2 * pair_rows // hour_devices
    far_share = pair_rows // hour_devices
    valid_f = jnp.repeat(validity.reshape(-1).astype(jnp.float32), comp_count)
    tile = jnp.broadcast_to(jnp.pad(valid_f, (0, 128 - trace_count))[None, :], (8, 128))
    near, far = pl.pallas_call(
        functools.partial(fused_kernel, (block_count, hour_devices)),
        out_shape=(
            jax.ShapeDtypeStruct((2, near_share, LAGS), jnp.float32),
            jax.ShapeDtypeStruct((far_share, LAGS), jnp.float32),
        ),
        in_specs=[pl.BlockSpec(memory_space=pltpu.VMEM)] * 3
        + [pl.BlockSpec(memory_space=pl.ANY)],
        out_specs=[pl.BlockSpec(memory_space=pltpu.VMEM)] * 2,
        scratch_shapes=[
            pltpu.VMEM(table.shape, jnp.bfloat16),
            pltpu.VMEM((3, part_count, trace_count, freq_count), jnp.bfloat16),
            pltpu.VMEM((part_count, trace_count + half, freq_count), jnp.float32),
            pltpu.VMEM((pair_rows, 2 * CHUNK), jnp.bfloat16),
            pltpu.VMEM((pair_rows, 2 * CHUNK), jnp.bfloat16),
            pltpu.VMEM((pair_rows, LAGS), jnp.float32),
            pltpu.VMEM((3, 8, 128), jnp.float32),
            pltpu.VMEM((hour_devices, 3, 8, 128), jnp.float32),
            pltpu.VMEM((2, 2, chips, near_share, LAGS), jnp.bfloat16),
            pltpu.VMEM((2, chips, far_share, LAGS), jnp.bfloat16),
            pltpu.VMEM((2, chips, near_share, LAGS), jnp.bfloat16),
            pltpu.VMEM((chips, far_share, LAGS), jnp.bfloat16),
            pltpu.VMEM((2, chips, near_share, LAGS), jnp.bfloat16),
            pltpu.VMEM((chips, far_share, LAGS), jnp.bfloat16),
            pltpu.VMEM((2, chips, near_share, LAGS), jnp.bfloat16),
            pltpu.VMEM((chips, far_share, LAGS), jnp.bfloat16),
            pltpu.SemaphoreType.DMA((4,)),
            pltpu.SemaphoreType.DMA((4,)),
            pltpu.SemaphoreType.DMA((2,)),
            pltpu.SemaphoreType.DMA,
            pltpu.SemaphoreType.DMA((2,)),
            pltpu.SemaphoreType.DMA((2,)),
            pltpu.SemaphoreType.DMA((hour_devices - 1,)),
            pltpu.SemaphoreType.DMA((hour_devices - 1,)),
            pltpu.SemaphoreType.DMA((5,)),
            pltpu.SemaphoreType.DMA((5,)),
            pltpu.SemaphoreType.DMA((3, chips)),
            pltpu.SemaphoreType.DMA((3, chips)),
        ],
        compiler_params=pltpu.CompilerParams(
            vmem_limit_bytes=48 * 1024 * 1024, collective_id=0, has_side_effects=True
        ),
    )(spectra.reshape(trace_count, part_count, freq_count), valid_f[:, None], tile, table)
    return near[None], far[None]


def solution(mesh):
    in_specs = (P("hours", "blocks", None, None, None), P("hours", "blocks"))
    out_specs = (P("blocks", None, "hours", None), P("blocks", "hours", None))

    def run(spectra, validity):
        table = chunked_table(spectra.shape[-1], LAGS)
        fits = mesh.shape["hours"] == 8 and mesh.shape["blocks"] == 4
        device_part = on_device_fused if fits else on_device
        return jax.shard_map(
            lambda *args: device_part(jnp.asarray(table), *args),
            mesh=mesh, in_specs=in_specs, out_specs=out_specs, check_vma=False,
        )(spectra, validity)

    return run
```

```python
import functools
import math

import jax
import jax.numpy as jnp
import ml_dtypes
import numpy as np
from jax import lax
from jax.experimental import pallas as pl
from jax.experimental.pallas import tpu as pltpu
from jax.sharding import PartitionSpec as P

BAND = 128
LAGS = 256
EPSILON = 1e-06
CHUNK = 256


def passed_along(block, axis, distance):
    devices = range(lax.axis_size(axis))
    route = [((i - distance) % len(devices), i) for i in devices]
    return lax.ppermute(block, axis, route)


def chunked_table(freq_count, lag_count):
    freq = np.arange(freq_count, dtype=np.int64)[:, None]
    lag = np.arange(lag_count, dtype=np.int64)[None, :] - lag_count // 2
    angles = ((freq * lag) % (2 * freq_count)).astype(np.float64) * (math.pi / freq_count)
    amplitude = 8.0 / math.sqrt(freq_count)
    parts = np.stack([np.cos(angles) * amplitude, -np.sin(angles) * amplitude], 0)
    parts = parts.reshape(2, freq_count // CHUNK, CHUNK, lag_count).transpose(1, 0, 2, 3)
    return parts.reshape(2 * freq_count, lag_count).astype(np.float32).astype(ml_dtypes.bfloat16)


def whiten_into(spectra_ref, valid_ref, store):
    freq_count = spectra_ref.shape[2]
    valid = valid_ref[...]
    for band in range(freq_count // BAND):
        lanes = slice(band * BAND, (band + 1) * BAND)
        real = spectra_ref[:, 0, lanes]
        imag = spectra_ref[:, 1, lanes]
        total = jnp.sum(real * real + imag * imag, axis=1, keepdims=True)
        scale = valid / jnp.sqrt(total * (1.0 / (2 * BAND)) + EPSILON)
        store(0, lanes, (real * scale).astype(jnp.bfloat16))
        store(1, lanes, (imag * scale).astype(jnp.bfloat16))


def whiten_kernel(spectra_ref, valid_ref, white_ref):
    def store(part, lanes, value):
        white_ref[part, :, lanes] = value

    whiten_into(spectra_ref, valid_ref, store)


def cross_chunk(rows_ref, row_start, row_count, cols_ref, panel, chunk, out_ref):
    col_count = cols_ref.shape[2]
    lanes = pl.ds(chunk * CHUNK, CHUNK)
    cols = [
        (
            cols_ref[panel, 0, q : q + 16, lanes],
            cols_ref[panel, 1, q : q + 16, lanes],
        )
        for q in range(0, col_count, 16)
    ]
    for a in range(row_count):
        row_real = jnp.broadcast_to(rows_ref[0, pl.ds(row_start + a, 1), lanes], (16, CHUNK))
        row_imag = jnp.broadcast_to(rows_ref[1, pl.ds(row_start + a, 1), lanes], (16, CHUNK))
        row_real = row_real.astype(jnp.bfloat16)
        row_imag = row_imag.astype(jnp.bfloat16)
        for q, (col_real, col_imag) in enumerate(cols):
            at = slice(a * col_count + q * 16, a * col_count + q * 16 + 16)
            out_ref[at, :CHUNK] = row_real * col_real + row_imag * col_imag
            out_ref[at, CHUNK:] = row_imag * col_real - row_real * col_imag


def correlate_unit(rows_ref, row_start, row_count, cols_ref, panel, table_ref, acc_ref, tiles):
    chunk_count = rows_ref.shape[2] // CHUNK
    cross = functools.partial(cross_chunk, rows_ref, row_start, row_count, cols_ref, panel)
    cross(0, tiles[0])
    for chunk in range(chunk_count):
        if chunk + 1 < chunk_count:
            cross(chunk + 1, tiles[(chunk + 1) % 2])
        term = jnp.dot(
            tiles[chunk % 2][...],
            table_ref[chunk * 2 * CHUNK : (chunk + 1) * 2 * CHUNK, :],
            preferred_element_type=jnp.float32,
        )
        if chunk == 0:
            acc_ref[...] = term
        else:
            acc_ref[...] += term


def correlate_kernel(block_count, white_ref, table_ref, out_ref, rows, tile0, tile1):
    trace_count = white_ref.shape[2]
    half = trace_count // 2
    is_lower = lax.axis_index("blocks") < block_count // 2
    rows[:, :trace_count, :] = white_ref[0].astype(jnp.float32)
    far_own = white_ref[0, :, :, :].astype(jnp.float32)[:, :half]
    far_other = white_ref[2, :, :, :].astype(jnp.float32)[:, half:]
    rows[:, trace_count:, :] = jnp.where(is_lower, far_own, far_other)

    def one_unit(unit, carry):
        near = unit < 4
        row_start = jnp.where(near, lax.rem(unit, 2) * half, trace_count)
        panel = jnp.where(near, unit // 2, jnp.where(is_lower, 2, 0))
        correlate_unit(
            rows, row_start, half, white_ref, panel, table_ref, out_ref.at[unit], (tile0, tile1)
        )
        return carry

    lax.fori_loop(0, 5, one_unit, 0)


def expand(counts, comp_count):
    return jnp.repeat(jnp.repeat(counts, comp_count, 0), comp_count, 1).reshape(-1)


def on_device(table, spectra, validity):
    hour_count, station_count, comp_count, part_count, freq_count = spectra.shape
    trace_count = station_count * comp_count
    half_width = trace_count // 2
    half_stations = station_count // 2
    block_count = lax.axis_size("blocks")
    near_rounds = block_count // 2
    my_block = lax.axis_index("blocks")
    is_lower = my_block < near_rounds
    valid_f = jnp.repeat(validity.reshape(-1).astype(jnp.float32), comp_count)[:, None]
    white = pl.pallas_call(
        whiten_kernel,
        out_shape=jax.ShapeDtypeStruct((part_count, trace_count, freq_count), jnp.bfloat16),
        in_specs=[pl.BlockSpec(memory_space=pltpu.VMEM)] * 2,
        out_specs=pl.BlockSpec(memory_space=pltpu.VMEM),
    )(spectra.reshape(trace_count, part_count, freq_count), valid_f)
    panels = [white] + [passed_along(white, "blocks", r) for r in range(1, near_rounds + 1)]
    pair_rows = half_width * trace_count
    sums = pl.pallas_call(
        functools.partial(correlate_kernel, block_count),
        out_shape=jax.ShapeDtypeStruct((5, pair_rows, LAGS), jnp.float32),
        in_specs=[pl.BlockSpec(memory_space=pltpu.VMEM)] * 2,
        out_specs=pl.BlockSpec(memory_space=pltpu.VMEM),
        scratch_shapes=[
            pltpu.VMEM((part_count, trace_count + half_width, freq_count), jnp.float32),
            pltpu.VMEM((pair_rows, 2 * CHUNK), jnp.bfloat16),
            pltpu.VMEM((pair_rows, 2 * CHUNK), jnp.bfloat16),
        ],
        compiler_params=pltpu.CompilerParams(vmem_limit_bytes=56 * 1024 * 1024),
    )(jnp.stack(panels, 0), table)
    near_terms = sums[:4].reshape(near_rounds, 2 * pair_rows, LAGS)
    far_terms = sums[4]
    hour_devices = lax.axis_size("hours")
    share_near = trace_count * trace_count // hour_devices
    share_far = half_width * trace_count // hour_devices
    my_slot = lax.axis_index("hours")
    hour_masks = lax.all_gather(validity, "hours", axis=0, tiled=True)
    all_masks = lax.all_gather(hour_masks, "blocks", axis=1, tiled=True).astype(jnp.float32)
    pair_counts = jnp.dot(
        all_masks.T, all_masks, precision=lax.Precision.HIGHEST, preferred_element_type=jnp.float32
    )
    near_sum, far_sum = (
        lax.psum_scatter(near_terms, "hours", scatter_dimension=1, tiled=True),
        lax.psum_scatter(far_terms, "hours", scatter_dimension=0, tiled=True),
    )

    def block_count_of(row_start, row_count, col_start):
        sub_block = lax.dynamic_slice(
            pair_counts, (row_start, col_start), (row_count, station_count)
        )
        return expand(sub_block, comp_count)

    near_full = jnp.stack(
        [
            block_count_of(
                my_block * station_count,
                station_count,
                (my_block - round_index) % block_count * station_count,
            )
            for round_index in range(near_rounds)
        ],
        0,
    )
    far_partner = (my_block + near_rounds) % block_count
    far_full = block_count_of(
        jnp.where(is_lower, my_block * station_count, far_partner * station_count + half_stations),
        half_stations,
        jnp.where(is_lower, far_partner, my_block) * station_count,
    )
    near_count = lax.dynamic_slice_in_dim(near_full, my_slot * share_near, share_near, 1)
    far_count = lax.dynamic_slice_in_dim(far_full, my_slot * share_far, share_far, 0)
    near_stack = near_sum / jnp.maximum(near_count, 1.0)[..., None]
    far_stack = far_sum / jnp.maximum(far_count, 1.0)[..., None]
    return (near_stack[None], far_stack[None])


def fused_kernel(
    sizes, spectra_ref, valid_ref, tile_ref, table_hbm, near_ref, far_ref,
    table_ref, white, rows, tile0, tile1, acc, masks, all_masks,
    near_part, far_part, near_sib, far_sib, near_pair, far_pair, near_in, far_in,
    z_send, z_recv, f_send, t_sem, m_send, m_recv, h_send, h_recv, s_send, s_recv,
    c_send, c_recv,
):
    block_count, hour_devices = sizes
    chips = hour_devices // 2
    trace_count = white.shape[2]
    half = trace_count // 2
    near_share = near_ref.shape[1]
    far_share = far_ref.shape[0]
    me = lax.axis_index("hours")
    block = lax.axis_index("blocks")
    core = lax.rem(me, 2)
    chip = me // 2
    other = 1 - core
    is_lower = block < block_count // 2
    following = lax.rem(block + 1, block_count)
    partner = lax.rem(block + 2, block_count)

    def remote(src, dst, send, recv, device):
        return pltpu.make_async_remote_copy(
            src_ref=src, dst_ref=dst, send_sem=send, recv_sem=recv,
            device_id=device, device_id_type=pl.DeviceIdType.MESH,
        )

    table_copy = pltpu.make_async_copy(table_hbm, table_ref, t_sem)
    table_copy.start()
    barrier = pltpu.get_barrier_semaphore()
    for step in range(1, hour_devices):
        pl.semaphore_signal(
            barrier, inc=1, device_id={"hours": lax.rem(me + step, hour_devices)},
            device_id_type=pl.DeviceIdType.MESH,
        )
    for step in range(1, block_count):
        pl.semaphore_signal(
            barrier, inc=1, device_id={"blocks": lax.rem(block + step, block_count)},
            device_id_type=pl.DeviceIdType.MESH,
        )

    def store(part, lanes, value):
        white[0, part, :, lanes] = value
        rows[part, :trace_count, lanes] = value.astype(jnp.float32)

    whiten_into(spectra_ref, valid_ref, store)
    masks[0] = tile_ref[...]
    pl.semaphore_wait(barrier, hour_devices + block_count - 2)

    mask_copies = [
        remote(masks.at[0], masks.at[i + 1], m_send.at[i], m_recv.at[i], {"blocks": to})
        for i, to in enumerate((following, partner))
    ]
    lead = half // 16 * 16
    upper_part = pl.ds(lead, trace_count - lead)
    parts = range(2)
    near_copies = [
        remote(
            white.at[0, p], white.at[1, p], z_send.at[p], z_recv.at[p], {"blocks": following}
        )
        for p in parts
    ]
    full_copies = [
        remote(
            white.at[0, p], white.at[2, p], z_send.at[2 + p], z_recv.at[2 + p],
            {"blocks": partner},
        )
        for p in parts
    ]
    half_copies = [
        remote(
            white.at[0, p, upper_part], white.at[2, p, upper_part],
            z_send.at[2 + p], z_recv.at[2 + p], {"blocks": partner},
        )
        for p in parts
    ]
    last = block == block_count - 1
    relay = block == 0
    relay_copies = [
        remote(
            white.at[1, p], white.at[2, p], f_send.at[p], z_recv.at[2 + p],
            {"blocks": following},
        )
        for p in parts
    ]
    for copy in mask_copies:
        copy.start()

    for copy in near_copies:
        copy.start()

    def relay_part(p):
        @pl.when(relay)
        def _():
            near_copies[p].wait_recv()
            relay_copies[p].start()

    table_copy.wait()

    def hour_copy(step):
        return remote(
            masks, all_masks.at[me], h_send.at[step - 1], h_recv.at[step - 1],
            {"hours": lax.rem(me + step, hour_devices)},
        )

    def sibling_near(unit):
        at = pl.ds((unit % 2) * (chips // 2), chips // 2)
        r = unit // 2
        return remote(
            near_part.at[r, other, at], near_sib.at[r, at],
            s_send.at[unit], s_recv.at[unit], {"hours": chip * 2 + other},
        )

    sibling_far = remote(
        far_part.at[other], far_sib, s_send.at[4], s_recv.at[4], {"hours": chip * 2 + other}
    )

    def chip_near(r, target):
        return remote(
            near_pair.at[r, target], near_in.at[r, chip],
            c_send.at[r, target], c_recv.at[r, chip], {"hours": target * 2 + core},
        )

    def chip_far(target):
        return remote(
            far_pair.at[target], far_in.at[chip],
            c_send.at[2, target], c_recv.at[2, chip], {"hours": target * 2 + core},
        )

    def reduce_near(unit):
        sibling_near(unit).wait_recv()
        r = unit // 2
        for i in range(chips // 2):
            target = (unit % 2) * (chips // 2) + i

            @pl.when(target != chip)
            def _():
                near_pair[r, target] = (
                    near_part[r, core, target].astype(jnp.float32)
                    + near_sib[r, target].astype(jnp.float32)
                ).astype(jnp.bfloat16)
                chip_near(r, target).start()

    def one_unit(unit, carry):
        near = unit < 4

        @pl.when(unit == 1)
        def _():
            relay_part(0)

        @pl.when(unit == 2)
        def _():
            relay_part(1)

            @pl.when(is_lower)
            def _():
                for copy in half_copies:
                    copy.start()

            @pl.when(jnp.logical_not(jnp.logical_or(is_lower, last)))
            def _():
                for copy in full_copies:
                    copy.start()

            for copy in mask_copies:
                copy.wait_recv()
            all_masks[me] = masks[...]
            for step in range(1, hour_devices):
                hour_copy(step).start()
            reduce_near(1)

            @pl.when(jnp.logical_not(relay))
            def _():
                for copy in near_copies:
                    copy.wait_recv()

        @pl.when(unit == 4)
        def _():
            reduce_near(3)

            @pl.when(is_lower)
            def _():
                for copy in full_copies:
                    copy.wait_recv()
                rows[:, trace_count:, :] = rows[:, :half, :]

            @pl.when(jnp.logical_not(is_lower))
            def _():
                for p in parts:
                    half_copies[p].wait_recv()
                    value = white[2, p, lead:, :].astype(jnp.float32)
                    rows[p, trace_count:, :] = value[half - lead :]

        row_start = jnp.where(near, lax.rem(unit, 2) * half, trace_count)
        panel = jnp.where(near, unit // 2, jnp.where(is_lower, 2, 0))
        correlate_unit(rows, row_start, half, white, panel, table_ref, acc, (tile0, tile1))

        @pl.when(near)
        def _():
            for i in range(hour_devices // 2):
                target = lax.rem(unit, 2) * (chips // 2) + i // 2
                near_part[unit // 2, i % 2, target] = acc[
                    i * near_share : (i + 1) * near_share, :
                ].astype(jnp.bfloat16)
            sibling_near(unit).start()

        @pl.when(jnp.logical_not(near))
        def _():
            for i in range(hour_devices):
                far_part[i % 2, i // 2] = acc[
                    i * far_share : (i + 1) * far_share, :
                ].astype(jnp.bfloat16)
            sibling_far.start()

        @pl.when(jnp.logical_or(unit == 1, unit == 3))
        def _():
            reduce_near(unit - 1)

        return carry

    lax.fori_loop(0, 5, one_unit, 0)

    sibling_far.wait_recv()
    for step in range(1, chips):
        target = lax.rem(chip + step, chips)
        far_pair[target] = (
            far_part[core, target].astype(jnp.float32) + far_sib[target].astype(jnp.float32)
        ).astype(jnp.bfloat16)
        chip_far(target).start()

    for step in range(1, hour_devices):
        hour_copy(step).wait()

    def counts(row_mask, row_start, row_count, col_mask):
        shape = (row_count, trace_count, 128)
        lane = lax.broadcasted_iota(jnp.int32, shape, 2)
        row = lax.broadcasted_iota(jnp.int32, shape, 0) + row_start
        col = lax.broadcasted_iota(jnp.int32, shape, 1)
        flat = (row_count * trace_count, 128)

        def picked(index, mask):
            chosen = jnp.where(lane == index, 1.0, 0.0).reshape(flat)
            return lax.dot_general(
                chosen, mask, (((1,), (1,)), ((), ())), preferred_element_type=jnp.float32
            )

        both = picked(row, row_mask) * picked(col, col_mask)
        return jnp.maximum(jnp.sum(both, axis=1, keepdims=True), 1.0)

    row_share = near_share // trace_count
    own_mask = all_masks[:, 0, 0, :]
    near_counts = [
        counts(own_mask, me * row_share, row_share, all_masks[:, r, 0, :]) for r in range(2)
    ]
    far_mask = all_masks[:, 2, 0, :]
    far_count = counts(
        jnp.where(is_lower, own_mask, far_mask),
        me * (row_share // 2) + jnp.where(is_lower, 0, half),
        row_share // 2,
        jnp.where(is_lower, far_mask, own_mask),
    )

    def chip_near_arrival(r, source):
        return remote(
            near_pair.at[r, source], near_in.at[r, source],
            c_send.at[r, source], c_recv.at[r, source], {"hours": source * 2 + core},
        )

    def chip_far_arrival(source):
        return remote(
            far_pair.at[source], far_in.at[source],
            c_send.at[2, source], c_recv.at[2, source], {"hours": source * 2 + core},
        )

    for r in range(2):
        total = near_part[r, core, chip].astype(jnp.float32) + near_sib[r, chip].astype(
            jnp.float32
        )
        for step in range(1, chips):
            source = lax.rem(chip + step, chips)
            chip_near_arrival(r, source).wait()
            total = total + near_in[r, source].astype(jnp.float32)
        near_ref[r] = total / near_counts[r]
    total = far_part[core, chip].astype(jnp.float32) + far_sib[chip].astype(jnp.float32)
    for step in range(1, chips):
        source = lax.rem(chip + step, chips)
        chip_far_arrival(source).wait()
        total = total + far_in[source].astype(jnp.float32)
    far_ref[...] = total / far_count

    for copy in mask_copies:
        copy.wait_send()

    for copy in near_copies:
        copy.wait_send()

    @pl.when(relay)
    def _():
        for copy in relay_copies:
            copy.wait_send()

    @pl.when(is_lower)
    def _():
        for copy in half_copies:
            copy.wait_send()

    @pl.when(jnp.logical_not(jnp.logical_or(is_lower, last)))
    def _():
        for copy in full_copies:
            copy.wait_send()

    for unit in range(4):
        sibling_near(unit).wait_send()
    sibling_far.wait_send()


def on_device_fused(table, spectra, validity):
    hour_count, station_count, comp_count, part_count, freq_count = spectra.shape
    trace_count = station_count * comp_count
    half = trace_count // 2
    block_count = lax.axis_size("blocks")
    hour_devices = lax.axis_size("hours")
    chips = hour_devices // 2
    pair_rows = half * trace_count
    near_share = 2 * pair_rows // hour_devices
    far_share = pair_rows // hour_devices
    valid_f = jnp.repeat(validity.reshape(-1).astype(jnp.float32), comp_count)
    tile = jnp.broadcast_to(jnp.pad(valid_f, (0, 128 - trace_count))[None, :], (8, 128))
    near, far = pl.pallas_call(
        functools.partial(fused_kernel, (block_count, hour_devices)),
        out_shape=(
            jax.ShapeDtypeStruct((2, near_share, LAGS), jnp.float32),
            jax.ShapeDtypeStruct((far_share, LAGS), jnp.float32),
        ),
        in_specs=[pl.BlockSpec(memory_space=pltpu.VMEM)] * 3
        + [pl.BlockSpec(memory_space=pl.ANY)],
        out_specs=[pl.BlockSpec(memory_space=pltpu.VMEM)] * 2,
        scratch_shapes=[
            pltpu.VMEM(table.shape, jnp.bfloat16),
            pltpu.VMEM((3, part_count, trace_count, freq_count), jnp.bfloat16),
            pltpu.VMEM((part_count, trace_count + half, freq_count), jnp.float32),
            pltpu.VMEM((pair_rows, 2 * CHUNK), jnp.bfloat16),
            pltpu.VMEM((pair_rows, 2 * CHUNK), jnp.bfloat16),
            pltpu.VMEM((pair_rows, LAGS), jnp.float32),
            pltpu.VMEM((3, 8, 128), jnp.float32),
            pltpu.VMEM((hour_devices, 3, 8, 128), jnp.float32),
            pltpu.VMEM((2, 2, chips, near_share, LAGS), jnp.bfloat16),
            pltpu.VMEM((2, chips, far_share, LAGS), jnp.bfloat16),
            pltpu.VMEM((2, chips, near_share, LAGS), jnp.bfloat16),
            pltpu.VMEM((chips, far_share, LAGS), jnp.bfloat16),
            pltpu.VMEM((2, chips, near_share, LAGS), jnp.bfloat16),
            pltpu.VMEM((chips, far_share, LAGS), jnp.bfloat16),
            pltpu.VMEM((2, chips, near_share, LAGS), jnp.bfloat16),
            pltpu.VMEM((chips, far_share, LAGS), jnp.bfloat16),
            pltpu.SemaphoreType.DMA((4,)),
            pltpu.SemaphoreType.DMA((4,)),
            pltpu.SemaphoreType.DMA((2,)),
            pltpu.SemaphoreType.DMA,
            pltpu.SemaphoreType.DMA((2,)),
            pltpu.SemaphoreType.DMA((2,)),
            pltpu.SemaphoreType.DMA((hour_devices - 1,)),
            pltpu.SemaphoreType.DMA((hour_devices - 1,)),
            pltpu.SemaphoreType.DMA((5,)),
            pltpu.SemaphoreType.DMA((5,)),
            pltpu.SemaphoreType.DMA((3, chips)),
            pltpu.SemaphoreType.DMA((3, chips)),
        ],
        compiler_params=pltpu.CompilerParams(
            vmem_limit_bytes=48 * 1024 * 1024, collective_id=0, has_side_effects=True
        ),
    )(spectra.reshape(trace_count, part_count, freq_count), valid_f[:, None], tile, table)
    return near[None], far[None]


def solution(mesh):
    in_specs = (P("hours", "blocks", None, None, None), P("hours", "blocks"))
    out_specs = (P("blocks", None, "hours", None), P("blocks", "hours", None))

    def run(spectra, validity):
        table = chunked_table(spectra.shape[-1], LAGS)
        fits = mesh.shape["hours"] == 8 and mesh.shape["blocks"] == 4
        device_part = on_device_fused if fits else on_device
        return jax.shard_map(
            lambda *args: device_part(jnp.asarray(table), *args),
            mesh=mesh, in_specs=in_specs, out_specs=out_specs, check_vma=False,
        )(spectra, validity)

    return run
```
